128 devices in a mesh: subj: 4 (over z_lo, core), blk: 32 (over y, x, z_hi).
Axes of the slice: x: 4, y: 4, z: 4 (z_hi: 2, z_lo: 2; z = z_hi * 2 + z_lo), core: 2. Of those that a mesh axis runs over, the one named last changes fastest.
Arguments:
- series: bfloat16 [8, 1200, 32768], P('subj', None, 'blk'), may hold values from -170 to 170
- circle_step: int32 [1], replicated, may hold values from 1 to 31
- vertex_count: int32 [32], replicated, may hold values from 1 to 1024, 28672 in all
Outputs:
- group_z: float32 [1024, 32768], P('subj', 'blk')
The draws below stay inside these ranges and needn't reach their ends.
Inputs may be any that keep to these rules, and one draw needn't show every extreme that they name: `vertex_count`: the counts sum to 28672.
All inputs are finite; a program needn't handle non-finite values.
Results may differ from the reference program's by a relative error of at most 0.0019.
Values may be sent and summed in bfloat16 or wider, within the bound.
No kernel may reach another device: no remote copies, remote signals or barrier semaphores. Data moves between devices by JAX's collectives and lax.ppermute only.
A program may use at most 192 MiB of HBM per device.

```python
import math
import jax
import jax.numpy as jnp
import numpy as np
from jax import lax

VB = 1024
FRAMES = 1200
SUBJECTS = 8
VERTS = 32768
N_BLK = 32


def draw_series(key, part):
    subkeys = jax.random.split(key, 5)
    full_shape = (SUBJECTS, FRAMES, VERTS)
    courses = jnp.clip(jax.random.normal(subkeys[0], (SUBJECTS, FRAMES, 2), jnp.float32), -4.0, 4.0)
    loadings = jax.random.uniform(subkeys[1], (SUBJECTS, 1, VERTS, 2), jnp.float32, -1.2, 1.2)
    noise = jnp.clip(jax.random.normal(subkeys[2], full_shape, jnp.float32), -4.0, 4.0)
    vertex_scale = jnp.exp(jax.random.uniform(subkeys[3], (SUBJECTS, 1, VERTS), jnp.float32, 0.0, math.log(10.0)))
    offset = jnp.clip(3.0 * jax.random.normal(subkeys[4], (SUBJECTS, 1, VERTS), jnp.float32), -9.0, 9.0)
    signal = courses[:, :, 0:1] * loadings[..., 0] + courses[:, :, 1:2] * loadings[..., 1] + noise
    return (signal * vertex_scale + offset).astype(jnp.bfloat16)


def split_up(number_of, total, reach, lean):
    loads = [(1 << 20) // math.isqrt(rank ** lean) + 1 for rank in range(2, number_of + 1)]
    surplus, holding = total - reach - (number_of - 1), [1] * (number_of - 1)
    while surplus > 0:
        movable = [i for i in range(number_of - 1) if holding[i] < reach]
        pool, budget = sum([loads[i] for i in movable]), surplus
        for i in movable:
            addition = min(reach - holding[i], max(1, budget * loads[i] // pool), surplus)
            holding[i] = holding[i] + addition
            surplus = surplus - addition
    return np.array([reach] + holding)


def ragged_sizes(key, count, total, reach, skew):
    if count == 2:
        one = jax.random.randint(key, (), max(1, total - reach), min(reach, total - 1) + 1)
        return jnp.stack([one, total - one])
    sizes = jnp.asarray(split_up(count, total, reach, skew), jnp.int32)
    twos = (count - 1) // 2
    giver, taker = sizes[1:1 + 2 * twos:2], sizes[2:2 + 2 * twos:2]
    room = jnp.minimum(giver - 1, reach - taker)
    shifted = jax.random.randint(jax.random.fold_in(key, 1), (twos,), 0, 1 << 20) % (room + 1)
    sizes = sizes.at[1:1 + 2 * twos:2].set(giver - shifted).at[2:2 + 2 * twos:2].set(taker + shifted)
    return sizes[jax.random.permutation(jax.random.fold_in(key, 2), count)]


def setup_inputs(seed: int = 0) -> dict:
    seeds = jax.random.split(jax.random.key(seed), 4)
    series = draw_series(jax.random.fold_in(seeds[3], 71), 0)
    circle_step = jax.random.randint(seeds[1], (1,), 1, N_BLK).astype(jnp.int32)
    vertex_count = ragged_sizes(seeds[2], N_BLK, N_BLK * VB - N_BLK * VB // 8, VB, 1).astype(jnp.int32)
    return {"series": series, "circle_step": circle_step, "vertex_count": vertex_count}


tr_seconds = 0.72
low_cut = 0.01
high_cut = 0.08
shrink = 0.98
epsilon = 1e-06

def tables(frames):
    index_row = jnp.arange(frames, dtype=jnp.int32)
    product_index = (2 * index_row[None, :] + 1) * index_row[:, None] % (4 * frames)
    phase_angle = product_index.astype(jnp.float32) * (math.pi / (2 * frames))
    row_scale = jnp.where(index_row == 0, math.sqrt(0.5), 1.0).astype(jnp.float32)
    cosine_table = jnp.cos(phase_angle) * math.sqrt(2.0 / frames) * row_scale[:, None]
    frequency = index_row.astype(jnp.float32) / (2 * frames * tr_seconds)
    high_pass = frequency / low_cut / jnp.sqrt(1.0 + (frequency / low_cut) ** 2)
    low_pass = 1.0 / jnp.sqrt(1.0 + (frequency / high_cut) ** 2)
    return (cosine_table.astype(jnp.bfloat16), (high_pass * low_pass)[:, None])

def normalize(raw_block, cosine_table, gains):
    coefficients = jnp.dot(cosine_table, raw_block, preferred_element_type=jnp.float32)
    weighted = (coefficients * gains).astype(jnp.bfloat16)
    filtered = jnp.dot(cosine_table.T, weighted, preferred_element_type=jnp.float32)
    frame_mean = lax.optimization_barrier(jnp.mean(filtered, axis=0, keepdims=True))
    centered = filtered - frame_mean
    variance = lax.optimization_barrier(jnp.mean(centered * centered, axis=0, keepdims=True))
    return (centered * lax.rsqrt(variance + epsilon)).astype(jnp.bfloat16)

def fisher(correlation):
    scaled = shrink * correlation
    return 0.5 * (jnp.log(1.0 + scaled) - jnp.log(1.0 - scaled))

def reference(series, circle_step, vertex_count):
    cosine_table, gains = tables(FRAMES)
    z_fields = jnp.stack([normalize(series[subject], cosine_table, gains) for subject in range(SUBJECTS)])
    shift_count = circle_step[0].astype(jnp.int32)

    def one_block(block):
        partner = ((block - shift_count) % N_BLK).astype(jnp.int32)
        own_z = lax.dynamic_slice_in_dim(z_fields, (block * VB).astype(jnp.int32), VB, 2)
        partner_z = lax.dynamic_slice_in_dim(z_fields, (partner * VB).astype(jnp.int32), VB, 2)
        running = jnp.zeros((VB, VB), jnp.float32)
        for subject in range(SUBJECTS):
            correlation = jnp.dot(partner_z[subject].T, own_z[subject], preferred_element_type=jnp.float32) / FRAMES
            running = running + fisher(correlation)
        slots = jnp.arange(VB, dtype=jnp.int32)
        keep_mask = (slots < vertex_count[partner])[:, None] & (slots < vertex_count[block])[None, :]
        return jnp.where(keep_mask, running / SUBJECTS, 0.0)
    tiles = lax.map(one_block, jnp.arange(N_BLK, dtype=jnp.int32))
    return jnp.transpose(tiles, (1, 0, 2)).reshape(VB, N_BLK * VB)
```

```python
import functools
import math

import jax
import jax.numpy as jnp
import numpy as np
from jax import lax
from jax.experimental import pallas as pl
from jax.experimental.pallas import tpu as pltpu
from jax.sharding import PartitionSpec as P

tr_seconds = 0.72
low_cut = 0.01
high_cut = 0.08
shrink = 0.98
epsilon = 1e-06
MIB = 1 << 20
TILE = 512


def tables(frames):
    index_row = np.arange(frames, dtype=np.int64)
    product_index = (2 * index_row[None, :] + 1) * index_row[:, None] % (4 * frames)
    phase_angle = product_index.astype(np.float32) * np.float32(math.pi / (2 * frames))
    row_scale = np.where(index_row == 0, math.sqrt(0.5), 1.0).astype(np.float32)
    cosine_table = np.cos(phase_angle.astype(np.float64)).astype(np.float32)
    cosine_table = cosine_table * np.float32(math.sqrt(2.0 / frames)) * row_scale[:, None]
    frequency = index_row.astype(np.float32) / np.float32(2 * frames * tr_seconds)
    high_pass = frequency / low_cut / np.sqrt(1.0 + (frequency / low_cut) ** 2)
    low_pass = 1.0 / np.sqrt(1.0 + (frequency / high_cut) ** 2)
    gains = (high_pass * low_pass).astype(np.float32)[:, None]
    return cosine_table.astype(jnp.bfloat16), gains


def normalize_kernel(series_ref, table_ref, turned_ref, gains_ref, z_ref):
    coefficients = jnp.dot(table_ref[...], series_ref[0], preferred_element_type=jnp.float32)
    weighted = (coefficients * gains_ref[...]).astype(jnp.bfloat16)
    filtered = jnp.dot(turned_ref[...], weighted, preferred_element_type=jnp.float32)
    frame_mean = jnp.mean(filtered, axis=0, keepdims=True)
    centered = filtered - frame_mean
    variance = jnp.mean(centered * centered, axis=0, keepdims=True)
    z_ref[0] = (centered * lax.rsqrt(variance + epsilon)).astype(jnp.bfloat16)


def normalize(series, consts):
    subjects, frames, width = series.shape
    table, turned, gains = consts
    whole = lambda shape: pl.BlockSpec(shape, lambda s, c: (0, 0))
    tile = pl.BlockSpec((1, frames, TILE), lambda s, c: (s, 0, c))
    return pl.pallas_call(
        normalize_kernel,
        grid=(subjects, width // TILE),
        in_specs=[tile, whole(table.shape), whole(turned.shape), whole(gains.shape)],
        out_specs=tile,
        out_shape=jax.ShapeDtypeStruct(series.shape, jnp.bfloat16),
        compiler_params=pltpu.CompilerParams(vmem_limit_bytes=56 * MIB),
        name="normalize",
    )(series, table, turned, gains)


def fisher_kernel(frames, partner_ref, own_ref, sum_ref):
    upper = lower = None
    for subject in range(partner_ref.shape[0]):
        scaled = lax.dot_general(
            partner_ref[subject],
            own_ref[subject],
            (((0,), (0,)), ((), ())),
            preferred_element_type=jnp.float32,
        ) * (shrink / frames)
        upper = 1.0 + scaled if subject == 0 else upper * (1.0 + scaled)
        lower = 1.0 - scaled if subject == 0 else lower * (1.0 - scaled)
    sum_ref[...] = 0.5 * (jnp.log(upper) - jnp.log(lower))


def fisher_sum(partner, own):
    subjects, frames, width = own.shape
    rows = partner.shape[2]
    high = rows // 4
    return pl.pallas_call(
        functools.partial(fisher_kernel, frames),
        grid=(rows // high, width // TILE),
        in_specs=[
            pl.BlockSpec((subjects, frames, high), lambda r, c: (0, 0, r)),
            pl.BlockSpec((subjects, frames, TILE), lambda r, c: (0, 0, c)),
        ],
        out_specs=pl.BlockSpec((high, TILE), lambda r, c: (r, c)),
        out_shape=jax.ShapeDtypeStruct((rows, width), jnp.float32),
        compiler_params=pltpu.CompilerParams(vmem_limit_bytes=56 * MIB),
        name="fisher",
    )(partner, own)


def scatter_sum(part, subj_index):
    rows, width = part.shape
    core = subj_index % 2
    z_half = subj_index // 2
    parts = part.reshape(2, 2, rows // 4, width)
    mine = lax.dynamic_index_in_dim(parts, core, 1, keepdims=False)
    other = lax.dynamic_index_in_dim(parts, 1 - core, 1, keepdims=False)
    near = mine + lax.ppermute(other, "subj", [(d, d ^ 1) for d in range(4)])
    mine = lax.dynamic_index_in_dim(near, z_half, 0, keepdims=False)
    other = lax.dynamic_index_in_dim(near, 1 - z_half, 0, keepdims=False)
    far = lax.ppermute(other.astype(jnp.bfloat16), "subj", [(d, d ^ 2) for d in range(4)])
    return mine + far.astype(jnp.float32)


def local(series, circle_step, vertex_count):
    subj_local, frames, width = series.shape
    table, gains = tables(frames)
    consts = (jnp.asarray(table), jnp.asarray(np.ascontiguousarray(table.T)), jnp.asarray(gains))
    shift_count = circle_step[0]
    block_total = lax.axis_size("blk")
    subj_total = lax.axis_size("subj")
    own_block = lax.axis_index("blk")
    subj_index = lax.axis_index("subj")
    partner = (own_block - shift_count) % block_total
    share = width // subj_total

    own = normalize(series, consts)

    def case(steps):
        pairs = [(source, (source + steps) % block_total) for source in range(block_total)]
        return lambda value: lax.ppermute(value, "blk", pairs)

    arrived = lax.switch(shift_count - 1, [case(steps) for steps in range(1, block_total)], own)
    summed = scatter_sum(fisher_sum(arrived, own), subj_index)

    block_ids = jnp.arange(block_total, dtype=jnp.int32)
    own_count = jnp.sum(jnp.where(block_ids == own_block, vertex_count, 0))
    partner_count = jnp.sum(jnp.where(block_ids == partner, vertex_count, 0))
    row_slots = subj_index * share + jnp.arange(share, dtype=jnp.int32)
    col_slots = jnp.arange(width, dtype=jnp.int32)
    keep_mask = (row_slots < partner_count)[:, None] & (col_slots < own_count)[None, :]
    return jnp.where(keep_mask, summed / (subj_local * subj_total), 0.0)


def solution(mesh):
    in_specs = (P("subj", None, "blk"), P(), P())
    out_specs = P("subj", "blk")
    return jax.shard_map(local, mesh=mesh, in_specs=in_specs, out_specs=out_specs, check_vma=False)
```

```python
import functools
import math

import jax
import jax.numpy as jnp
import numpy as np
from jax import lax
from jax.experimental import pallas as pl
from jax.experimental.pallas import tpu as pltpu
from jax.sharding import PartitionSpec as P

tr_seconds = 0.72
low_cut = 0.01
high_cut = 0.08
shrink = 0.98
epsilon = 1e-06
LIMIT = 60 << 20
LANES = 128
TILE = 512
STRIP = 256


def tables(frames):
    index_row = np.arange(frames, dtype=np.int64)
    product_index = (2 * index_row[None, :] + 1) * index_row[:, None] % (4 * frames)
    phase_angle = product_index.astype(np.float32) * np.float32(math.pi / (2 * frames))
    row_scale = np.where(index_row == 0, math.sqrt(0.5), 1.0).astype(np.float32)
    cosine_table = np.cos(phase_angle.astype(np.float64)).astype(np.float32)
    cosine_table = cosine_table * np.float32(math.sqrt(2.0 / frames)) * row_scale[:, None]
    cosine_table = cosine_table.astype(jnp.bfloat16)
    frequency = index_row.astype(np.float32) / np.float32(2 * frames * tr_seconds)
    high_pass = frequency / low_cut / np.sqrt(1.0 + (frequency / low_cut) ** 2)
    low_pass = 1.0 / np.sqrt(1.0 + (frequency / high_cut) ** 2)
    gains = (high_pass * low_pass).astype(np.float32)[:, None]
    half = frames // 2
    analysis = np.zeros((2, half, padded(frames)), cosine_table.dtype)
    synthesis = np.zeros((2, half, padded(half)), cosine_table.dtype)
    for parity in range(2):
        analysis[parity, :, :frames] = cosine_table[parity::2]
        synthesis[parity, :, :half] = cosine_table[parity::2, :half].T
    return analysis, synthesis, np.stack([gains[0::2], gains[1::2]])


def padded(count):
    return -(-count // LANES) * LANES


def normalize_kernel(series_ref, analysis_ref, synthesis_ref, gains_ref, z_ref, raw):
    frames, tile = series_ref.shape[1:]
    half = frames // 2
    raw[:frames] = series_ref[0]
    raw[frames:] = jnp.zeros((raw.shape[0] - frames, tile), raw.dtype)
    parts = []
    for parity in range(2):
        coefficients = jnp.dot(analysis_ref[parity], raw[...], preferred_element_type=jnp.float32)
        weighted = coefficients * gains_ref[parity]
        blank = jnp.zeros((synthesis_ref.shape[2] - half, tile), jnp.float32)
        weighted = jnp.concatenate([weighted, blank], axis=0).astype(jnp.bfloat16)
        parts.append(jnp.dot(synthesis_ref[parity], weighted, preferred_element_type=jnp.float32))
    even, odd = parts
    frame_mean = jnp.sum(even, axis=0, keepdims=True) * (2.0 / frames)
    early = even + odd - frame_mean
    late = even - odd - frame_mean
    squares = jnp.sum(early * early, axis=0, keepdims=True) + jnp.sum(late * late, axis=0, keepdims=True)
    scale = lax.rsqrt(squares / frames + epsilon)
    early, late = early * scale, late * scale
    whole = half // 16 * 16
    z_ref[0, :whole] = early[:whole].astype(jnp.bfloat16)
    z_ref[0, whole : 2 * whole] = late[:whole].astype(jnp.bfloat16)
    rest = jnp.concatenate([early[whole:], late[whole:]], axis=0)
    z_ref[0, 2 * whole :] = rest.astype(jnp.bfloat16)


def normalize(series, consts):
    subjects, frames, width = series.shape
    whole = lambda array: pl.BlockSpec(array.shape, lambda s, c: (0, 0, 0))
    tile = pl.BlockSpec((1, frames, TILE), lambda s, c: (s, 0, c))
    return pl.pallas_call(
        normalize_kernel,
        grid=(subjects, width // TILE),
        in_specs=[tile, *map(whole, consts)],
        out_specs=tile,
        out_shape=jax.ShapeDtypeStruct(series.shape, jnp.bfloat16),
        scratch_shapes=[pltpu.VMEM((padded(frames), TILE), jnp.bfloat16)],
        compiler_params=pltpu.CompilerParams(vmem_limit_bytes=LIMIT),
        name="normalize",
    )(series, *consts)


def fisher_kernel(frames, place_ref, partner_ref, own_ref, near_ref, kept_ref):
    subjects, _, width = own_ref.shape

    def columns(start):
        upper = lower = None
        for subject in range(subjects):
            scaled = lax.dot_general(
                partner_ref[subject],
                own_ref[subject, :, start : start + STRIP],
                (((0,), (0,)), ((), ())),
                preferred_element_type=jnp.float32,
            ) * (shrink / frames)
            upper = 1.0 + scaled if subject == 0 else upper * (1.0 + scaled)
            lower = 1.0 - scaled if subject == 0 else lower * (1.0 - scaled)
        return 0.5 * jnp.log(upper / lower)

    sums = [columns(start) for start in range(0, width, STRIP)]
    for core, sum_ref in enumerate((near_ref, kept_ref)):

        @pl.when(pl.program_id(0) == core)
        def _():
            for strip, value in enumerate(sums):
                sum_ref[:, strip * STRIP : (strip + 1) * STRIP] = value


def fisher_sum(partner, own, z_half, core):
    subjects, frames, width = own.shape
    share = width // 4
    place = jnp.stack([2 * z_half + 1 - core, 2 * z_half + core])
    out = jax.ShapeDtypeStruct((share, width), jnp.float32)
    return pl.pallas_call(
        functools.partial(fisher_kernel, frames),
        grid_spec=pltpu.PrefetchScalarGridSpec(
            num_scalar_prefetch=1,
            grid=(2,),
            in_specs=[
                pl.BlockSpec((subjects, frames, share), lambda r, place: (0, 0, place[r])),
                pl.BlockSpec((subjects, frames, width), lambda r, place: (0, 0, 0)),
            ],
            out_specs=[pl.BlockSpec((share, width), lambda r, place: (0, 0))] * 2,
        ),
        out_shape=[out, out],
        compiler_params=pltpu.CompilerParams(vmem_limit_bytes=LIMIT),
        cost_estimate=pl.CostEstimate(flops=1, bytes_accessed=1, transcendentals=0),
        name="fisher",
    )(place, partner, own)


def local(series, circle_step, vertex_count):
    subj_local, frames, width = series.shape
    consts = tuple(jnp.asarray(value) for value in tables(frames))
    shift_count = circle_step[0]
    block_total = lax.axis_size("blk")
    subj_total = lax.axis_size("subj")
    own_block = lax.axis_index("blk")
    subj_index = lax.axis_index("subj")
    z_half, core = subj_index // 2, subj_index % 2
    partner = (own_block - shift_count) % block_total
    share = width // subj_total

    own = normalize(series, consts)

    def case(steps):
        pairs = [(source, (source + steps) % block_total) for source in range(block_total)]
        return lambda value: lax.ppermute(value, "blk", pairs)

    arrived = lax.switch(shift_count - 1, [case(steps) for steps in range(1, block_total)], own)

    def to_other_core(value):
        return lax.ppermute(value, "subj", [(d, d ^ 1) for d in range(4)])

    near, kept = fisher_sum(arrived, own, 1 - z_half, core)
    leaving = (kept + to_other_core(near)).astype(jnp.bfloat16)
    leaving, z_half = lax.optimization_barrier((leaving, z_half))
    far = lax.ppermute(leaving, "subj", [(d, d ^ 2) for d in range(4)])
    near, kept = fisher_sum(arrived, own, z_half, core)
    near, far = lax.optimization_barrier((near, far))
    summed = kept + to_other_core(near) + far.astype(jnp.float32)

    block_ids = jnp.arange(block_total, dtype=jnp.int32)
    own_count = jnp.sum(jnp.where(block_ids == own_block, vertex_count, 0))
    partner_count = jnp.sum(jnp.where(block_ids == partner, vertex_count, 0))
    row_slots = subj_index * share + jnp.arange(share, dtype=jnp.int32)
    col_slots = jnp.arange(width, dtype=jnp.int32)
    keep_mask = (row_slots < partner_count)[:, None] & (col_slots < own_count)[None, :]
    return jnp.where(keep_mask, summed / (subj_local * subj_total), 0.0)


def solution(mesh):
    in_specs = (P("subj", None, "blk"), P(), P())
    out_specs = P("subj", "blk")
    return jax.shard_map(local, mesh=mesh, in_specs=in_specs, out_specs=out_specs, check_vma=False)
```

```python
import functools
import math

import jax
import jax.numpy as jnp
import numpy as np
from jax import lax
from jax.experimental import pallas as pl
from jax.experimental.pallas import tpu as pltpu
from jax.sharding import PartitionSpec as P

tr_seconds = 0.72
low_cut = 0.01
high_cut = 0.08
shrink = 0.98
epsilon = 1e-06
LIMIT = 60 << 20
FISHER_LIMIT = 40 << 20
LANES = 128
TILE = 512
STRIP = 256


def tables(frames):
    index_row = np.arange(frames, dtype=np.int64)
    product_index = (2 * index_row[None, :] + 1) * index_row[:, None] % (4 * frames)
    phase_angle = product_index.astype(np.float32) * np.float32(math.pi / (2 * frames))
    row_scale = np.where(index_row == 0, math.sqrt(0.5), 1.0).astype(np.float32)
    cosine_table = np.cos(phase_angle.astype(np.float64)).astype(np.float32)
    cosine_table = cosine_table * np.float32(math.sqrt(2.0 / frames)) * row_scale[:, None]
    cosine_table = cosine_table.astype(jnp.bfloat16)
    frequency = index_row.astype(np.float32) / np.float32(2 * frames * tr_seconds)
    high_pass = frequency / low_cut / np.sqrt(1.0 + (frequency / low_cut) ** 2)
    low_pass = 1.0 / np.sqrt(1.0 + (frequency / high_cut) ** 2)
    gains = (high_pass * low_pass).astype(np.float32)[:, None]
    half = frames // 2
    analysis = np.zeros((2, half, padded(frames)), cosine_table.dtype)
    synthesis = np.zeros((2, half, padded(half)), cosine_table.dtype)
    for parity in range(2):
        analysis[parity, :, :frames] = cosine_table[parity::2]
        synthesis[parity, :, :half] = cosine_table[parity::2, :half].T
    return analysis, synthesis, np.stack([gains[0::2], gains[1::2]])


def padded(count):
    return -(-count // LANES) * LANES


def normalize_kernel(series_ref, analysis_ref, synthesis_ref, gains_ref, z_ref, raw):
    frames, tile = series_ref.shape[1:]
    half = frames // 2
    raw[:frames] = series_ref[0]
    raw[frames:] = jnp.zeros((raw.shape[0] - frames, tile), raw.dtype)
    parts = []
    for parity in range(2):
        coefficients = jnp.dot(analysis_ref[parity], raw[...], preferred_element_type=jnp.float32)
        weighted = coefficients * gains_ref[parity]
        blank = jnp.zeros((synthesis_ref.shape[2] - half, tile), jnp.float32)
        weighted = jnp.concatenate([weighted, blank], axis=0).astype(jnp.bfloat16)
        parts.append(jnp.dot(synthesis_ref[parity], weighted, preferred_element_type=jnp.float32))
    even, odd = parts
    frame_mean = jnp.sum(even, axis=0, keepdims=True) * (2.0 / frames)
    early = even + odd - frame_mean
    late = even - odd - frame_mean
    squares = jnp.sum(early * early, axis=0, keepdims=True) + jnp.sum(late * late, axis=0, keepdims=True)
    scale = lax.rsqrt(squares / frames + epsilon)
    early, late = early * scale, late * scale
    whole = half // 16 * 16
    z_ref[0, :whole] = early[:whole].astype(jnp.bfloat16)
    z_ref[0, whole : 2 * whole] = late[:whole].astype(jnp.bfloat16)
    rest = jnp.concatenate([early[whole:], late[whole:]], axis=0)
    z_ref[0, 2 * whole :] = rest.astype(jnp.bfloat16)


def normalize(series, consts):
    subjects, frames, width = series.shape
    whole = lambda array: pl.BlockSpec(array.shape, lambda s, c: (0, 0, 0))
    tile = pl.BlockSpec((1, frames, TILE), lambda s, c: (s, 0, c))
    return pl.pallas_call(
        normalize_kernel,
        grid=(subjects, width // TILE),
        in_specs=[tile, *map(whole, consts)],
        out_specs=tile,
        out_shape=jax.ShapeDtypeStruct(series.shape, jnp.bfloat16),
        scratch_shapes=[pltpu.VMEM((padded(frames), TILE), jnp.bfloat16)],
        compiler_params=pltpu.CompilerParams(vmem_limit_bytes=LIMIT),
        name="normalize",
    )(series, *consts)


def fisher_kernel(frames, place_ref, partner_ref, own_ref, near_ref, kept_ref):
    subjects, _, width = own_ref.shape

    def columns(start):
        upper = lower = None
        for subject in range(subjects):
            scaled = lax.dot_general(
                partner_ref[subject],
                own_ref[subject, :, start : start + STRIP],
                (((0,), (0,)), ((), ())),
                preferred_element_type=jnp.float32,
            ) * (shrink / frames)
            upper = 1.0 + scaled if subject == 0 else upper * (1.0 + scaled)
            lower = 1.0 - scaled if subject == 0 else lower * (1.0 - scaled)
        return 0.5 * jnp.log(upper / lower)

    sums = [columns(start) for start in range(0, width, STRIP)]
    for core, sum_ref in enumerate((near_ref, kept_ref)):

        @pl.when(pl.program_id(0) == core)
        def _():
            for strip, value in enumerate(sums):
                sum_ref[:, strip * STRIP : (strip + 1) * STRIP] = value


def fisher_sum(partner, own, place):
    subjects, frames, width = own.shape
    share = width // 4
    out = jax.ShapeDtypeStruct((share, width), jnp.float32)
    return pl.pallas_call(
        functools.partial(fisher_kernel, frames),
        grid_spec=pltpu.PrefetchScalarGridSpec(
            num_scalar_prefetch=1,
            grid=(2,),
            in_specs=[
                pl.BlockSpec((subjects, frames, share), lambda r, place: (0, 0, place[r])),
                pl.BlockSpec((subjects, frames, width), lambda r, place: (0, 0, 0)),
            ],
            out_specs=[pl.BlockSpec((share, width), lambda r, place: (0, 0))] * 2,
        ),
        out_shape=[out, out],
        compiler_params=pltpu.CompilerParams(vmem_limit_bytes=FISHER_LIMIT),
        cost_estimate=pl.CostEstimate(flops=1, bytes_accessed=1, transcendentals=0),
        name="fisher",
    )(place, partner, own)


def local(series, circle_step, vertex_count):
    subj_local, frames, width = series.shape
    consts = tuple(jnp.asarray(value) for value in tables(frames))
    shift_count = circle_step[0]
    block_total = lax.axis_size("blk")
    subj_total = lax.axis_size("subj")
    own_block = lax.axis_index("blk")
    subj_index = lax.axis_index("subj")
    places = subj_index ^ jnp.array([3, 2, 1, 0], jnp.int32)
    other_chip, this_chip = places[:2], places[2:]
    partner = (own_block - shift_count) % block_total
    share = width // subj_total

    own = normalize(series, consts)

    def case(steps):
        pairs = [(source, (source + steps) % block_total) for source in range(block_total)]
        return lambda value: lax.ppermute(value, "blk", pairs)

    arrived = lax.switch(shift_count - 1, [case(steps) for steps in range(1, block_total)], own)

    def to_other_core(value):
        return lax.ppermute(value, "subj", [(d, d ^ 1) for d in range(4)])

    near, kept = fisher_sum(arrived, own, other_chip)
    leaving = (kept + to_other_core(near)).astype(jnp.bfloat16)
    leaving, this_chip = lax.optimization_barrier((leaving, this_chip))
    far = lax.ppermute(leaving, "subj", [(d, d ^ 2) for d in range(4)])
    near, kept = fisher_sum(arrived, own, this_chip)
    near, far = lax.optimization_barrier((near, far))
    summed = kept + to_other_core(near) + far.astype(jnp.float32)

    block_ids = jnp.arange(block_total, dtype=jnp.int32)
    own_count = jnp.sum(jnp.where(block_ids == own_block, vertex_count, 0))
    partner_count = jnp.sum(jnp.where(block_ids == partner, vertex_count, 0))
    row_slots = subj_index * share + jnp.arange(share, dtype=jnp.int32)
    col_slots = jnp.arange(width, dtype=jnp.int32)
    keep_mask = (row_slots < partner_count)[:, None] & (col_slots < own_count)[None, :]
    return jnp.where(keep_mask, summed / (subj_local * subj_total), 0.0)


def solution(mesh):
    in_specs = (P("subj", None, "blk"), P(), P())
    out_specs = P("subj", "blk")
    return jax.shard_map(local, mesh=mesh, in_specs=in_specs, out_specs=out_specs, check_vma=False)
```

```python
import functools
import math

import jax
import jax.numpy as jnp
import numpy as np
from jax import lax
from jax.experimental import pallas as pl
from jax.experimental.pallas import tpu as pltpu
from jax.sharding import PartitionSpec as P

tr_seconds = 0.72
low_cut = 0.01
high_cut = 0.08
shrink = 0.98
epsilon = 1e-06
LIMIT = 60 << 20
FISHER_LIMIT = 40 << 20
LANES = 128
TILE = 512
STRIP = 256


def tables(frames):
    index_row = np.arange(frames, dtype=np.int64)
    product_index = (2 * index_row[None, :] + 1) * index_row[:, None] % (4 * frames)
    phase_angle = product_index.astype(np.float32) * np.float32(math.pi / (2 * frames))
    row_scale = np.where(index_row == 0, math.sqrt(0.5), 1.0).astype(np.float32)
    cosine_table = np.cos(phase_angle.astype(np.float64)).astype(np.float32)
    cosine_table = cosine_table * np.float32(math.sqrt(2.0 / frames)) * row_scale[:, None]
    cosine_table = cosine_table.astype(jnp.bfloat16)
    frequency = index_row.astype(np.float32) / np.float32(2 * frames * tr_seconds)
    high_pass = frequency / low_cut / np.sqrt(1.0 + (frequency / low_cut) ** 2)
    low_pass = 1.0 / np.sqrt(1.0 + (frequency / high_cut) ** 2)
    gains = (high_pass * low_pass).astype(np.float32)[:, None]
    half = frames // 2
    analysis = np.zeros((2, half, padded(frames)), cosine_table.dtype)
    synthesis = np.zeros((2, half, padded(half)), cosine_table.dtype)
    for parity in range(2):
        analysis[parity, :, :frames] = cosine_table[parity::2]
        synthesis[parity, :, :half] = cosine_table[parity::2, :half].T
    return analysis, synthesis, np.stack([gains[0::2], gains[1::2]])


def padded(count):
    return -(-count // LANES) * LANES


def normalize_kernel(series_ref, analysis_ref, synthesis_ref, gains_ref, z_ref, raw):
    frames, tile = series_ref.shape[1:]
    half = frames // 2
    raw[:frames] = series_ref[0]
    raw[frames:] = jnp.zeros((raw.shape[0] - frames, tile), raw.dtype)
    parts = []
    for parity in range(2):
        coefficients = jnp.dot(analysis_ref[parity], raw[...], preferred_element_type=jnp.float32)
        weighted = coefficients * gains_ref[parity]
        blank = jnp.zeros((synthesis_ref.shape[2] - half, tile), jnp.float32)
        weighted = jnp.concatenate([weighted, blank], axis=0).astype(jnp.bfloat16)
        parts.append(jnp.dot(synthesis_ref[parity], weighted, preferred_element_type=jnp.float32))
    even, odd = parts
    frame_mean = jnp.sum(even, axis=0, keepdims=True) * (2.0 / frames)
    early = even + odd - frame_mean
    late = even - odd - frame_mean
    squares = jnp.sum(early * early, axis=0, keepdims=True) + jnp.sum(late * late, axis=0, keepdims=True)
    scale = lax.rsqrt(squares / frames + epsilon)
    early, late = early * scale, late * scale
    whole = half // 16 * 16
    z_ref[0, :whole] = early[:whole].astype(jnp.bfloat16)
    z_ref[0, whole : 2 * whole] = late[:whole].astype(jnp.bfloat16)
    rest = jnp.concatenate([early[whole:], late[whole:]], axis=0)
    z_ref[0, 2 * whole :] = rest.astype(jnp.bfloat16)


def normalize(series, consts):
    subjects, frames, width = series.shape
    whole = lambda array: pl.BlockSpec(array.shape, lambda s, c: (0, 0, 0))
    tile = pl.BlockSpec((1, frames, TILE), lambda s, c: (s, 0, c))
    return pl.pallas_call(
        normalize_kernel,
        grid=(subjects, width // TILE),
        in_specs=[tile, *map(whole, consts)],
        out_specs=tile,
        out_shape=jax.ShapeDtypeStruct(series.shape, jnp.bfloat16),
        scratch_shapes=[pltpu.VMEM((padded(frames), TILE), jnp.bfloat16)],
        compiler_params=pltpu.CompilerParams(vmem_limit_bytes=LIMIT),
        name="normalize",
    )(series, *consts)


def fisher_kernel(frames, place_ref, partner_ref, own_ref, near_ref, kept_ref):
    subjects, _, width = own_ref.shape

    def columns(start):
        upper = lower = None
        for subject in range(subjects):
            scaled = lax.dot_general(
                partner_ref[subject],
                own_ref[subject, :, start : start + STRIP],
                (((0,), (0,)), ((), ())),
                preferred_element_type=jnp.float32,
            ) * (shrink / frames)
            upper = 1.0 + scaled if subject == 0 else upper * (1.0 + scaled)
            lower = 1.0 - scaled if subject == 0 else lower * (1.0 - scaled)
        return 0.5 * jnp.log(upper / lower)

    sums = [columns(start) for start in range(0, width, STRIP)]
    for core, sum_ref in enumerate((near_ref, kept_ref)):

        @pl.when(pl.program_id(0) == core)
        def _():
            for strip, value in enumerate(sums):
                sum_ref[:, strip * STRIP : (strip + 1) * STRIP] = value


def fisher_sum(partner, own, place, chip):
    subjects, frames, width = own.shape
    share = width // 4
    out = jax.ShapeDtypeStruct((share, width), jnp.float32)
    return pl.pallas_call(
        functools.partial(fisher_kernel, frames),
        grid_spec=pltpu.PrefetchScalarGridSpec(
            num_scalar_prefetch=1,
            grid=(2,),
            in_specs=[
                pl.BlockSpec((subjects, frames, share), lambda r, place: (0, 0, place[0] ^ (2 * chip + 1 - r))),
                pl.BlockSpec((subjects, frames, width), lambda r, place: (0, 0, 0)),
            ],
            out_specs=[pl.BlockSpec((share, width), lambda r, place: (0, 0))] * 2,
        ),
        out_shape=[out, out],
        compiler_params=pltpu.CompilerParams(vmem_limit_bytes=FISHER_LIMIT),
        cost_estimate=pl.CostEstimate(flops=1, bytes_accessed=1, transcendentals=0),
        name="fisher",
    )(place[None], partner, own)


def local(series, circle_step, vertex_count):
    subj_local, frames, width = series.shape
    consts = tuple(jnp.asarray(value) for value in tables(frames))
    shift_count = circle_step[0]
    block_total = lax.axis_size("blk")
    subj_total = lax.axis_size("subj")
    own_block = lax.axis_index("blk")
    subj_index = lax.axis_index("subj")
    partner = (own_block - shift_count) % block_total
    share = width // subj_total

    own = normalize(series, consts)

    def case(steps):
        pairs = [(source, (source + steps) % block_total) for source in range(block_total)]
        return lambda value: lax.ppermute(value, "blk", pairs)

    arrived = lax.switch(shift_count - 1, [case(steps) for steps in range(1, block_total)], own)

    def to_other_core(value):
        return lax.ppermute(value, "subj", [(d, d ^ 1) for d in range(4)])

    near, kept = fisher_sum(arrived, own, subj_index, 1)
    leaving = (kept + to_other_core(near)).astype(jnp.bfloat16)
    leaving, place = lax.optimization_barrier((leaving, subj_index))
    far = lax.ppermute(leaving, "subj", [(d, d ^ 2) for d in range(4)])
    near, kept = fisher_sum(arrived, own, place, 0)
    near, far = lax.optimization_barrier((near, far))
    near = to_other_core(near)
    kept, near = lax.optimization_barrier((kept + far.astype(jnp.float32), near))
    summed = kept + near

    block_ids = jnp.arange(block_total, dtype=jnp.int32)
    own_count = jnp.sum(jnp.where(block_ids == own_block, vertex_count, 0))
    partner_count = jnp.sum(jnp.where(block_ids == partner, vertex_count, 0))
    row_slots = subj_index * share + jnp.arange(share, dtype=jnp.int32)
    col_slots = jnp.arange(width, dtype=jnp.int32)
    keep_mask = (row_slots < partner_count)[:, None] & (col_slots < own_count)[None, :]
    return jnp.where(keep_mask, summed / (subj_local * subj_total), 0.0)


def solution(mesh):
    in_specs = (P("subj", None, "blk"), P(), P())
    out_specs = P("subj", "blk")
    return jax.shard_map(local, mesh=mesh, in_specs=in_specs, out_specs=out_specs, check_vma=False)
```

```python
import functools
import math

import jax
import jax.numpy as jnp
import numpy as np
from jax import lax
from jax.experimental import pallas as pl
from jax.experimental.pallas import tpu as pltpu
from jax.sharding import PartitionSpec as P

tr_seconds = 0.72
low_cut = 0.01
high_cut = 0.08
shrink = 0.98
epsilon = 1e-06
LIMIT = 60 << 20
FISHER_LIMIT = 40 << 20
LANES = 128
TILE = 1024
STRIP = 256


def tables(frames):
    index_row = np.arange(frames, dtype=np.int64)
    product_index = (2 * index_row[None, :] + 1) * index_row[:, None] % (4 * frames)
    phase_angle = product_index.astype(np.float32) * np.float32(math.pi / (2 * frames))
    row_scale = np.where(index_row == 0, math.sqrt(0.5), 1.0).astype(np.float32)
    cosine_table = np.cos(phase_angle.astype(np.float64)).astype(np.float32)
    cosine_table = cosine_table * np.float32(math.sqrt(2.0 / frames)) * row_scale[:, None]
    cosine_table = cosine_table.astype(jnp.bfloat16)
    frequency = index_row.astype(np.float32) / np.float32(2 * frames * tr_seconds)
    high_pass = frequency / low_cut / np.sqrt(1.0 + (frequency / low_cut) ** 2)
    low_pass = 1.0 / np.sqrt(1.0 + (frequency / high_cut) ** 2)
    gains = (high_pass * low_pass).astype(np.float32)[:, None]
    half = frames // 2
    analysis = np.zeros((2, half, padded(frames)), cosine_table.dtype)
    synthesis = np.zeros((2, half, padded(half)), cosine_table.dtype)
    for parity in range(2):
        analysis[parity, :, :frames] = cosine_table[parity::2]
        synthesis[parity, :, :half] = cosine_table[parity::2, :half].T
    return analysis, synthesis, np.stack([gains[0::2], gains[1::2]])


def padded(count):
    return -(-count // LANES) * LANES


def normalize_kernel(series_ref, analysis_ref, synthesis_ref, gains_ref, z_ref, raw):
    frames, tile = series_ref.shape[1:]
    half = frames // 2
    raw[:frames] = series_ref[0]
    raw[frames:] = jnp.zeros((raw.shape[0] - frames, tile), raw.dtype)
    parts = []
    for parity in range(2):
        coefficients = jnp.dot(analysis_ref[parity], raw[...], preferred_element_type=jnp.float32)
        weighted = coefficients * gains_ref[parity]
        blank = jnp.zeros((synthesis_ref.shape[2] - half, tile), jnp.float32)
        weighted = jnp.concatenate([weighted, blank], axis=0).astype(jnp.bfloat16)
        parts.append(jnp.dot(synthesis_ref[parity], weighted, preferred_element_type=jnp.float32))
    even, odd = parts
    frame_mean = jnp.sum(even, axis=0, keepdims=True) * (2.0 / frames)
    early = even + odd - frame_mean
    late = even - odd - frame_mean
    squares = jnp.sum(early * early, axis=0, keepdims=True) + jnp.sum(late * late, axis=0, keepdims=True)
    scale = lax.rsqrt(squares / frames + epsilon)
    early, late = early * scale, late * scale
    whole = half // 16 * 16
    z_ref[0, :whole] = early[:whole].astype(jnp.bfloat16)
    z_ref[0, whole : 2 * whole] = late[:whole].astype(jnp.bfloat16)
    rest = jnp.concatenate([early[whole:], late[whole:]], axis=0)
    z_ref[0, 2 * whole :] = rest.astype(jnp.bfloat16)


def normalize(series, consts):
    subjects, frames, width = series.shape
    whole = lambda array: pl.BlockSpec(array.shape, lambda s, c: (0, 0, 0))
    tile = pl.BlockSpec((1, frames, TILE), lambda s, c: (s, 0, c))
    return pl.pallas_call(
        normalize_kernel,
        grid=(subjects, width // TILE),
        in_specs=[tile, *map(whole, consts)],
        out_specs=tile,
        out_shape=jax.ShapeDtypeStruct(series.shape, jnp.bfloat16),
        scratch_shapes=[pltpu.VMEM((padded(frames), TILE), jnp.bfloat16)],
        compiler_params=pltpu.CompilerParams(vmem_limit_bytes=LIMIT),
        name="normalize",
    )(series, *consts)


def fisher_kernel(frames, place_ref, partner_ref, own_ref, near_ref, kept_ref):
    subjects, _, width = own_ref.shape

    def columns(start):
        upper = lower = None
        for subject in range(subjects):
            scaled = lax.dot_general(
                partner_ref[subject],
                own_ref[subject, :, start : start + STRIP],
                (((0,), (0,)), ((), ())),
                preferred_element_type=jnp.float32,
            ) * (shrink / frames)
            upper = 1.0 + scaled if subject == 0 else upper * (1.0 + scaled)
            lower = 1.0 - scaled if subject == 0 else lower * (1.0 - scaled)
        return 0.5 * jnp.log(upper / lower)

    sums = [columns(start) for start in range(0, width, STRIP)]
    for core, sum_ref in enumerate((near_ref, kept_ref)):

        @pl.when(pl.program_id(0) == core)
        def _():
            for strip, value in enumerate(sums):
                sum_ref[:, strip * STRIP : (strip + 1) * STRIP] = value


def fisher_sum(partner, own, place, chip):
    subjects, frames, width = own.shape
    share = width // 4
    out = jax.ShapeDtypeStruct((share, width), jnp.float32)
    return pl.pallas_call(
        functools.partial(fisher_kernel, frames),
        grid_spec=pltpu.PrefetchScalarGridSpec(
            num_scalar_prefetch=1,
            grid=(2,),
            in_specs=[
                pl.BlockSpec((subjects, frames, share), lambda r, place: (0, 0, place[0] ^ (2 * chip + 1 - r))),
                pl.BlockSpec((subjects, frames, width), lambda r, place: (0, 0, 0)),
            ],
            out_specs=[pl.BlockSpec((share, width), lambda r, place: (0, 0))] * 2,
        ),
        out_shape=[out, out],
        compiler_params=pltpu.CompilerParams(vmem_limit_bytes=FISHER_LIMIT),
        cost_estimate=pl.CostEstimate(flops=1, bytes_accessed=1, transcendentals=0),
        name="fisher",
    )(place[None], partner, own)


def local(series, circle_step, vertex_count):
    subj_local, frames, width = series.shape
    consts = tuple(jnp.asarray(value) for value in tables(frames))
    shift_count = circle_step[0]
    block_total = lax.axis_size("blk")
    subj_total = lax.axis_size("subj")
    own_block = lax.axis_index("blk")
    subj_index = lax.axis_index("subj")
    partner = (own_block - shift_count) % block_total
    share = width // subj_total

    own = normalize(series, consts)

    def case(steps):
        pairs = [(source, (source + steps) % block_total) for source in range(block_total)]
        return lambda value: lax.ppermute(value, "blk", pairs)

    arrived = lax.switch(shift_count - 1, [case(steps) for steps in range(1, block_total)], own)

    def to_other_core(value):
        return lax.ppermute(value, "subj", [(d, d ^ 1) for d in range(4)])

    near, kept = fisher_sum(arrived, own, subj_index, 1)
    leaving = (kept + to_other_core(near)).astype(jnp.bfloat16)
    leaving, place = lax.optimization_barrier((leaving, subj_index))
    far = lax.ppermute(leaving, "subj", [(d, d ^ 2) for d in range(4)])
    near, kept = fisher_sum(arrived, own, place, 0)
    block_ids = jnp.arange(block_total, dtype=jnp.int32)
    own_count = jnp.sum(jnp.where(block_ids == own_block, vertex_count, 0))
    partner_count = jnp.sum(jnp.where(block_ids == partner, vertex_count, 0))
    near, far, own_count, partner_count = lax.optimization_barrier((near, far, own_count, partner_count))
    near = to_other_core(near)
    kept, near = lax.optimization_barrier((kept + far.astype(jnp.float32), near))
    summed = kept + near

    row_slots = subj_index * share + jnp.arange(share, dtype=jnp.int32)
    col_slots = jnp.arange(width, dtype=jnp.int32)
    keep_mask = (row_slots < partner_count)[:, None] & (col_slots < own_count)[None, :]
    return jnp.where(keep_mask, summed / (subj_local * subj_total), 0.0)


def solution(mesh):
    in_specs = (P("subj", None, "blk"), P(), P())
    out_specs = P("subj", "blk")
    return jax.shard_map(local, mesh=mesh, in_specs=in_specs, out_specs=out_specs, check_vma=False)
```
